256 devices in a mesh: head: 4 (over y_hi, core), blk: 64 (over z, x, y_lo).
Axes of the slice: x: 4, y: 4 (y_hi: 2, y_lo: 2; y = y_hi * 2 + y_lo), z: 8, core: 2. Of those that a mesh axis runs over, the one named last changes fastest.
Arguments:
- queries: bfloat16 [32768, 5120], P(('head', 'blk')), may hold values from -120 to 120
- keys: bfloat16 [32768, 5120], P(('head', 'blk')), may hold values from -120 to 120
- values: bfloat16 [32768, 5120], P(('head', 'blk')), may hold values from -6 to 6
- queries_tan: bfloat16 [32768, 5120], P(('head', 'blk')), may hold values from -6 to 6
- keys_tan: bfloat16 [32768, 5120], P(('head', 'blk')), may hold values from -6 to 6
- values_tan: bfloat16 [32768, 5120], P(('head', 'blk')), may hold values from -6 to 6
Outputs:
- attended: bfloat16 [32768, 5120], P(('head', 'blk'))
- attended_tan: bfloat16 [32768, 5120], P(('head', 'blk'))
- log_total: float32 [32768, 40], P(('head', 'blk'))
- log_total_tan: float32 [32768, 40], P(('head', 'blk'))
The draws below stay inside these ranges and needn't reach their ends.
All inputs are finite; a program needn't handle non-finite values.
Results may differ from the reference program's by a relative error of at most 0.005.
Values may be sent and summed in bfloat16 or wider, within the bound.
No kernel may reach another device: no remote copies, remote signals or barrier semaphores. Data moves between devices by JAX's collectives and lax.ppermute only.
A program may use at most 128 MiB of HBM per device.

```python
import jax
import jax.numpy as jnp
from jax import lax

H = 40
DH = 128
TOK_BLK = 512
D = 5120
BLOCKS = 64
TOKENS = 32768
PIECE = 128
N_HEAD = 4


def draw_queries(key, part):
    key = jax.random.fold_in(key, 11)
    result = jnp.clip(jax.random.normal(key, (TOKENS, H * DH), jnp.float32), -4.0, 4.0)
    return result.astype(jnp.bfloat16)


def draw_keys(key, part):
    key = jax.random.fold_in(key, 12)
    result = jnp.clip(jax.random.normal(key, (TOKENS, H * DH), jnp.float32), -4.0, 4.0)
    return result.astype(jnp.bfloat16)


def shard_levels(key, extent, split, smallest, high):
    level, own = 1.0, jax.random.fold_in(key, 6)
    for dim, parts in split:
        steps = jnp.exp(jax.random.uniform(jax.random.fold_in(own, dim), (parts,), jnp.float32, smallest / len(split), high / len(split)))
        level = level * jnp.repeat(steps, extent[dim] // parts).reshape([-1 if axis == dim else 1 for axis in range(len(extent))])
    return level


def gaussian(stream_key, dims, scale, limit, split=(), kind=jnp.bfloat16):
    loudness = shard_levels(stream_key, dims, split, -0.22, 0.18) if split else 1.0
    array = jax.random.normal(stream_key, dims, jnp.float32) * scale * loudness
    return jnp.minimum(jnp.maximum(array, -limit), limit).astype(kind)


def setup_inputs(seed: int = 0) -> dict:
    splits = jax.random.split(jax.random.key(seed), 7)
    queries = draw_queries(jax.random.fold_in(splits[6], 71), 0)
    keys = draw_keys(jax.random.fold_in(splits[6], 71), 0)
    values = gaussian(splits[2], (TOKENS, D), 1.0, 6.0, ((0, 256),))
    queries_tan = gaussian(splits[3], (TOKENS, D), 1.0, 6.0, ((0, 256),))
    keys_tan = gaussian(splits[4], (TOKENS, D), 1.0, 6.0, ((0, 256),))
    values_tan = gaussian(splits[5], (TOKENS, D), 1.0, 6.0, ((0, 256),))
    return {"queries": queries, "keys": keys, "values": values, "queries_tan": queries_tan, "keys_tan": keys_tan, "values_tan": values_tan}


def arrange(whole):
    return whole.reshape(N_HEAD, BLOCKS, PIECE, H, DH).transpose(1, 0, 2, 3, 4).reshape(BLOCKS, TOK_BLK, H, DH)


def restore(blocks_out, width):
    return blocks_out.reshape(BLOCKS, N_HEAD, PIECE, width).transpose(1, 0, 2, 3).reshape(TOKENS, width)


def reference(queries, keys, values, queries_tan, keys_tan, values_tan):
    query_rows = arrange(queries)
    query_tan = arrange(queries_tan)
    key_rows = arrange(keys)
    key_tan = arrange(keys_tan)
    value_rows = arrange(values)
    value_tan = arrange(values_tan)
    score_scale = 1.0 / (DH ** 0.5)

    def one_block(block_index):
        chosen = jnp.stack([(block_index - 1) % BLOCKS, block_index, (block_index + 1) % BLOCKS]).astype(jnp.int32)
        own_q = query_rows[block_index].astype(jnp.float32)
        own_dq = query_tan[block_index].astype(jnp.float32)
        near_k = key_rows[chosen].reshape(3 * TOK_BLK, H, DH).astype(jnp.float32)
        near_dk = key_tan[chosen].reshape(3 * TOK_BLK, H, DH).astype(jnp.float32)
        near_v = value_rows[chosen].reshape(3 * TOK_BLK, H, DH).astype(jnp.float32)
        near_dv = value_tan[chosen].reshape(3 * TOK_BLK, H, DH).astype(jnp.float32)
        scores = jnp.einsum("thd,khd->htk", own_q, near_k) * score_scale
        tangent_scores = (jnp.einsum("thd,khd->htk", own_dq, near_k) + jnp.einsum("thd,khd->htk", own_q, near_dk)) * score_scale
        row_max = jnp.max(scores, axis=-1, keepdims=True)
        expo = jnp.exp(scores - row_max)
        row_sum = jnp.sum(expo, axis=-1, keepdims=True)
        probs = expo / row_sum
        log_total = (row_max + jnp.log(row_sum))[..., 0]
        log_total_tan = jnp.sum(probs * tangent_scores, axis=-1)
        probs_tan = probs * (tangent_scores - log_total_tan[..., None])
        probs_low = probs.astype(jnp.bfloat16).astype(jnp.float32)
        probs_tan_low = probs_tan.astype(jnp.bfloat16).astype(jnp.float32)
        attended = jnp.einsum("htk,khd->thd", probs_low, near_v)
        attended_tan = jnp.einsum("htk,khd->thd", probs_tan_low, near_v) + jnp.einsum("htk,khd->thd", probs_low, near_dv)
        return (attended.reshape(TOK_BLK, H * DH).astype(jnp.bfloat16), attended_tan.reshape(TOK_BLK, H * DH).astype(jnp.bfloat16), log_total.T, log_total_tan.T)

    outs_a, outs_b, stats_a, stats_b = lax.map(one_block, jnp.arange(BLOCKS, dtype=jnp.int32))
    return (restore(outs_a, H * DH), restore(outs_b, H * DH), restore(stats_a, H), restore(stats_b, H))
```

```python
import functools

import jax
import jax.numpy as jnp
from jax import lax
from jax.experimental import pallas as pl
from jax.experimental.pallas import tpu as pltpu
from jax.sharding import Mesh, PartitionSpec as P

DH = 128
SEG = 128
GROUP = 8
BLK = 512
ROWS = 256
OUT_ROWS = 2 * SEG + 16
SCALE = 1.0 / DH**0.5
LOG2E = 1.4426950408889634
AXES = ("y_hi", "core", "z", "x", "y_lo")
RING = ("y_lo", "y_hi", "core")
LINE = ("z", "x")
CHUNKS = (2, 2, 1)


def pack(arrays, base, nh):
    width = nh * DH

    def body(q, k, v, dq, dk, dv, q_out, kv_out):
        for j in range(nh):
            cols = pl.ds(j * DH, DH)
            q_out[:, pl.ds((2 * j) * DH, DH)] = dq[:, cols]
            q_out[:, pl.ds((2 * j + 1) * DH, DH)] = q[:, cols]
            kv_out[:, pl.ds((4 * j) * DH, DH)] = k[:, cols]
            kv_out[:, pl.ds((4 * j + 1) * DH, DH)] = dk[:, cols]
            kv_out[:, pl.ds((4 * j + 2) * DH, DH)] = v[:, cols]
            kv_out[:, pl.ds((4 * j + 3) * DH, DH)] = dv[:, cols]

    first = base // nh
    spec = pl.BlockSpec((SEG, width), lambda d: (0, first + d))
    return pl.pallas_call(
        body,
        grid=(GROUP,),
        in_specs=[spec] * 6,
        out_specs=[
            pl.BlockSpec((SEG, 2 * width), lambda d: (d, 0)),
            pl.BlockSpec((SEG, 4 * width), lambda d: (d, 0)),
        ],
        out_shape=[
            jax.ShapeDtypeStruct((GROUP * SEG, 2 * width), jnp.bfloat16),
            jax.ShapeDtypeStruct((GROUP * SEG, 4 * width), jnp.bfloat16),
        ],
        cost_estimate=pl.CostEstimate(flops=0, bytes_accessed=24 * GROUP * SEG * width, transcendentals=0),
        name="pack",
    )(*arrays)


def attend_rows(q_ref, row, key_refs):
    joined_q = q_ref[pl.ds(row, ROWS), :]
    plain_q = joined_q[:, DH:]
    nt = (((1,), (1,)), ((), ()))
    scores, tangents = [], []
    for ref, rows in key_refs:
        joined_k = ref[:, 0 : 2 * DH]
        scores.append(lax.dot_general(plain_q, joined_k[:, :DH], nt, preferred_element_type=jnp.float32))
        tangents.append(lax.dot_general(joined_q, joined_k, nt, preferred_element_type=jnp.float32))
    top = functools.reduce(jnp.maximum, [jnp.max(s, axis=-1, keepdims=True) for s in scores])
    expo = [jnp.exp2((s - top) * (SCALE * LOG2E)) for s in scores]
    total = sum(jnp.sum(e, axis=-1, keepdims=True) for e in expo)
    mean = sum(jnp.sum(e * t, axis=-1, keepdims=True) for e, t in zip(expo, tangents)) / total
    both = jnp.zeros((ROWS, 2 * DH), jnp.float32)
    slope = jnp.zeros((ROWS, DH), jnp.float32)
    for (ref, rows), e, t in zip(key_refs, expo, tangents):
        low = e.astype(jnp.bfloat16)
        tan_low = (e * (t - mean)).astype(jnp.bfloat16)
        both = both + jnp.dot(low, ref[:, 2 * DH : 4 * DH], preferred_element_type=jnp.float32)
        slope = slope + jnp.dot(tan_low, ref[:, 2 * DH : 3 * DH], preferred_element_type=jnp.float32)
    inverse = 1.0 / total
    attended = both[:, :DH] * inverse
    attended_tan = (both[:, DH:] + slope * SCALE) * inverse
    log_total = top * SCALE + jnp.log(total)
    log_total_tan = mean * SCALE
    return attended, attended_tan, log_total, log_total_tan


def split3(x):
    high = x.astype(jnp.bfloat16)
    rest = x - high.astype(jnp.float32)
    middle = rest.astype(jnp.bfloat16)
    low = (rest - middle.astype(jnp.float32)).astype(jnp.bfloat16)
    return high, middle, low


def attention(q, kv, before, after, nh):
    def body(q_ref, kv_ref, before_ref, after_ref, out_ref):
        for half, far in enumerate((before_ref, after_ref)):
            for part in range(BLK // ROWS):
                row = half * BLK + part * ROWS
                attended, attended_tan, log_total, log_total_tan = attend_rows(
                    q_ref, row, ((kv_ref, 2 * BLK), (far, BLK))
                )
                lane = lax.broadcasted_iota(jnp.int32, (ROWS, DH), 1)
                stats = jnp.where(lane == 0, log_total, jnp.where(lane == 1, log_total_tan, 0.0))
                stats = jnp.concatenate([part_.astype(jnp.float32) for part_ in split3(stats)], axis=0)
                for s in range(ROWS // SEG):
                    d = row // SEG + s
                    here = slice(s * SEG, (s + 1) * SEG)
                    out_ref[d, 0:SEG, :] = attended[here].astype(jnp.bfloat16)
                    out_ref[d, SEG : 2 * SEG, :] = attended_tan[here].astype(jnp.bfloat16)
                    lines = [stats[p * ROWS + s * SEG : p * ROWS + (s + 1) * SEG].T[0:2] for p in range(3)]
                    lines.append(jnp.zeros((10, SEG), jnp.float32))
                    out_ref[d, 2 * SEG : OUT_ROWS, :] = jnp.concatenate(lines, axis=0).astype(jnp.bfloat16)

    width = 4 * DH
    return pl.pallas_call(
        body,
        grid=(nh,),
        in_specs=[
            pl.BlockSpec((2 * BLK, 2 * DH), lambda h: (0, h)),
            pl.BlockSpec((2 * BLK, width), lambda h: (0, h)),
            pl.BlockSpec((BLK, width), lambda h: (0, h)),
            pl.BlockSpec((BLK, width), lambda h: (0, h)),
        ],
        out_specs=pl.BlockSpec((GROUP, OUT_ROWS, DH), lambda h: (0, 0, h)),
        out_shape=jax.ShapeDtypeStruct((GROUP, OUT_ROWS, nh * DH), jnp.bfloat16),
        compiler_params=pltpu.CompilerParams(vmem_limit_bytes=48 * 1024 * 1024),
        cost_estimate=pl.CostEstimate(
            flops=nh * 2 * 16 * BLK * 3 * BLK * DH, bytes_accessed=nh * 6_000_000, transcendentals=nh * 6 * BLK * BLK
        ),
        name="attention",
    )(q, kv, before, after)


def unpack(chunks, plan):
    def body(*refs):
        parts, (att, att_tan, log_total, log_total_tan) = refs[: len(plan)], refs[len(plan) :]
        lines = []
        for ref, (base, nh) in zip(parts, plan):
            for s in range(GROUP):
                cols = pl.ds((base + s * nh) * DH, nh * DH)
                att[:, cols] = ref[s, 0:SEG, :]
                att_tan[:, cols] = ref[s, SEG : 2 * SEG, :]
                stat = ref[s, 2 * SEG : OUT_ROWS, :].astype(jnp.float32)
                stat = stat[0:2] + (stat[2:4] + stat[4:6])
                lines += [stat[:, j * DH : (j + 1) * DH] for j in range(nh)]
        pad = [jnp.zeros((2 * DH - 2 * len(lines), SEG), jnp.float32)]
        first = jnp.concatenate([line[0:1] for line in lines] + [jnp.zeros((DH - len(lines), SEG), jnp.float32)], axis=0)
        second = jnp.concatenate([line[1:2] for line in lines] + [jnp.zeros((DH - len(lines), SEG), jnp.float32)], axis=0)
        log_total[...] = first.T[:, : len(lines)]
        log_total_tan[...] = second.T[:, : len(lines)]

    heads = GROUP * sum(nh for _, nh in plan)
    return pl.pallas_call(
        body,
        out_shape=[
            jax.ShapeDtypeStruct((SEG, heads * DH), jnp.bfloat16),
            jax.ShapeDtypeStruct((SEG, heads * DH), jnp.bfloat16),
            jax.ShapeDtypeStruct((SEG, heads), jnp.float32),
            jax.ShapeDtypeStruct((SEG, heads), jnp.float32),
        ],
        compiler_params=pltpu.CompilerParams(vmem_limit_bytes=32 * 1024 * 1024),
        cost_estimate=pl.CostEstimate(flops=0, bytes_accessed=4 * SEG * heads * DH * 2, transcendentals=0),
        name="unpack",
    )(*chunks)


def exchange(rows):
    return lax.all_to_all(rows, RING, split_axis=0, concat_axis=0, tiled=True)


def along_line(rows, by, length):
    return lax.ppermute(rows, LINE, [(i, (i + by) % length) for i in range(length)])


def per_device(queries, keys, values, queries_tan, keys_tan, values_tan):
    arrays = (queries, keys, values, queries_tan, keys_tan, values_tan)
    length = lax.axis_size("z") * lax.axis_size("x")
    plan, base = [], 0
    for nh in CHUNKS:
        plan.append((base, nh))
        base += GROUP * nh
    returned = []
    for base, nh in plan:
        q, kv = pack(arrays, base, nh)
        kv = exchange(kv)
        q = exchange(q)
        before = along_line(kv[BLK:], 1, length)
        after = along_line(kv[:BLK], -1, length)
        out = attention(q, kv, before, after, nh)
        returned.append(exchange(out))
    return tuple(unpack(returned, plan))


def solution(mesh):
    inner = Mesh(mesh.devices.reshape(2, 2, 8, 4, 2), AXES)
    placed = P(AXES, None)
    return jax.shard_map(
        per_device,
        mesh=inner,
        in_specs=(placed,) * 6,
        out_specs=(placed,) * 4,
        check_vma=False,
    )
```

```python
import functools

import jax
import jax.numpy as jnp
from jax import lax
from jax.experimental import pallas as pl
from jax.experimental.pallas import tpu as pltpu
from jax.sharding import Mesh, PartitionSpec as P

DH = 128
SEG = 128
BLK = 512
ROWS = 256
SLOTS = 4
OUT_ROWS = 2 * SEG + 16
SCALE = 1.0 / DH**0.5
LOG2E = 1.4426950408889634
AXES = ("y_hi", "core", "z", "x", "y_lo")
RING = ("y_hi", "core", "y_lo")
LINE = ("core", "z", "x")
STEPS = ((1, 2, 3, 0), (2, 3, 0, 1))
CHUNKS = (4, 4, 2)
WINDOW = 4
GATHER = False
ORDER = (
    ("pack", 0),
    ("pack", 0),
    ("pack", 0),
    ("pack", 0),
    ("pack", 0),
    ("pack", 0),
    ("pack", 0),
    ("pack", 0),
    ("join", 0),
    ("pack", 0),
    ("pack", 0),
    ("pack", 0),
    ("pack", 0),
    ("join", 1),
    ("attend", 0),
    ("join", 2),
    ("attend", 1),
    ("attend", 2),
)
ANY = pl.BlockSpec(memory_space=pl.ANY)
HBM = pl.BlockSpec(memory_space=pltpu.HBM)
VMEM = pl.BlockSpec(memory_space=pltpu.VMEM)
MIB = 1024 * 1024


def slot_chip(k):
    y = 2 * lax.axis_index("y_hi") + lax.axis_index("y_lo")
    return (y + jnp.where(lax.axis_index("core") == 0, STEPS[0][k], STEPS[1][k])) % 4


def slot_pairs(k):
    pairs = []
    for y_hi in range(2):
        for core in range(2):
            for y_lo in range(2):
                y = (2 * y_hi + y_lo + STEPS[core][k]) % 4
                pairs.append((4 * y_hi + 2 * core + y_lo, 4 * (y // 2) + 2 * y_lo + y % 2))
    return pairs


def outer_pairs(length):
    return [(length + s, (s + 1) % length) for s in range(length)] + [
        (s, length + (s - 1) % length) for s in range(length)
    ]


def pack(arrays, base, nh, k, after):
    width = nh * DH

    def body(*refs):
        ins, (out, held, into, out_of) = refs[:6], refs[6 + len(after) :]
        first = pl.multiple_of((base + slot_chip(k) * nh) * DH, DH)
        loads = []
        for i, ref in enumerate(ins):
            load = pltpu.make_async_copy(
                ref.at[:, pl.ds(first, width)], held.at[:, pl.ds(i * width, width)], into.at[i]
            )
            load.start()
            loads.append(load)
        for load in loads:
            load.wait()
        store = pltpu.make_async_copy(held, out, out_of)
        store.start()
        store.wait()

    return pl.pallas_call(
        body,
        in_specs=[HBM] * 6 + [ANY] * len(after),
        out_specs=ANY,
        out_shape=jax.ShapeDtypeStruct((SEG, 6 * width), jnp.bfloat16),
        scratch_shapes=[
            pltpu.VMEM((SEG, 6 * width), jnp.bfloat16),
            pltpu.SemaphoreType.DMA((6,)),
            pltpu.SemaphoreType.DMA,
        ],
        compiler_params=pltpu.CompilerParams(vmem_limit_bytes=(16 if base else 60) * MIB),
        cost_estimate=pl.CostEstimate(flops=0, bytes_accessed=24 * SEG * width, transcendentals=0),
        name="pack",
    )(*arrays, *after)


def join(messages, nh, after):
    width = 4 * nh * DH

    def body(*refs):
        out = refs[-1]
        for k in range(SLOTS):
            out[k * SEG : (k + 1) * SEG, :] = refs[k][:, 2 * nh * DH :]

    return pl.pallas_call(
        body,
        in_specs=[VMEM] * SLOTS + [ANY] * len(after),
        out_specs=VMEM,
        out_shape=jax.ShapeDtypeStruct((BLK, width), jnp.bfloat16),
        compiler_params=pltpu.CompilerParams(vmem_limit_bytes=16 * MIB),
        cost_estimate=pl.CostEstimate(flops=0, bytes_accessed=4 * BLK * width, transcendentals=0),
        name="join",
    )(*messages, *after)


def attend_rows(plain_q, joined_q, key_refs):
    nt = (((1,), (1,)), ((), ()))
    scores, tangents = [], []
    for k, dk, v, dv in key_refs:
        plain_k = k[...]
        joined_k = jnp.concatenate([plain_k, dk[...]], axis=1)
        scores.append(lax.dot_general(plain_q, plain_k, nt, preferred_element_type=jnp.float32))
        tangents.append(lax.dot_general(joined_q, joined_k, nt, preferred_element_type=jnp.float32))
    top = functools.reduce(jnp.maximum, [jnp.max(s, axis=-1, keepdims=True) for s in scores])
    expo = [jnp.exp2((s - top) * (SCALE * LOG2E)) for s in scores]
    total = sum(jnp.sum(e, axis=-1, keepdims=True) for e in expo)
    mean = sum(jnp.sum(e * t, axis=-1, keepdims=True) for e, t in zip(expo, tangents)) / total
    both = jnp.zeros((ROWS, 2 * DH), jnp.float32)
    slope = jnp.zeros((ROWS, DH), jnp.float32)
    for (k, dk, v, dv), e, t in zip(key_refs, expo, tangents):
        low = e.astype(jnp.bfloat16)
        tan_low = (e * (t - mean)).astype(jnp.bfloat16)
        joined_v = jnp.concatenate([v[...], dv[...]], axis=1)
        both = both + jnp.dot(low, joined_v, preferred_element_type=jnp.float32)
        slope = slope + jnp.dot(tan_low, v[...], preferred_element_type=jnp.float32)
    inverse = 1.0 / total
    attended = both[:, :DH] * inverse
    attended_tan = (both[:, DH:] + slope * SCALE) * inverse
    log_total = top * SCALE + jnp.log(total)
    log_total_tan = mean * SCALE
    return attended, attended_tan, log_total, log_total_tan


def split3(x):
    high = x.astype(jnp.bfloat16)
    rest = x - high.astype(jnp.float32)
    middle = rest.astype(jnp.bfloat16)
    low = (rest - middle.astype(jnp.float32)).astype(jnp.bfloat16)
    return high, middle, low


def attention(messages, keysets, nh, after):
    def body(*refs):
        tan_refs, q_refs, refs = refs[:SLOTS], refs[SLOTS : 2 * SLOTS], refs[2 * SLOTS :]
        key_refs = [refs[4 * i : 4 * i + 4] for i in range(len(keysets))]
        outs = refs[4 * len(keysets) + len(after) :]
        per = ROWS // SEG
        for part in range(BLK // ROWS):
            here = range(part * per, part * per + per)
            plain_q = jnp.concatenate([q_refs[k][...] for k in here], axis=0)
            tan_q = jnp.concatenate([tan_refs[k][...] for k in here], axis=0)
            joined_q = jnp.concatenate([tan_q, plain_q], axis=1)
            attended, attended_tan, log_total, log_total_tan = attend_rows(plain_q, joined_q, key_refs)
            lane = lax.broadcasted_iota(jnp.int32, (ROWS, DH), 1)
            stats = jnp.where(lane == 0, log_total, jnp.where(lane == 1, log_total_tan, 0.0))
            pieces = [piece.astype(jnp.float32) for piece in split3(stats)]
            for s, k in enumerate(here):
                rows = slice(s * SEG, (s + 1) * SEG)
                outs[k][0:SEG, :] = attended[rows].astype(jnp.bfloat16)
                outs[k][SEG : 2 * SEG, :] = attended_tan[rows].astype(jnp.bfloat16)
                lines = [piece[rows].T[0:2] for piece in pieces]
                lines.append(jnp.zeros((10, SEG), jnp.float32))
                outs[k][2 * SEG : OUT_ROWS, :] = jnp.concatenate(lines, axis=0).astype(jnp.bfloat16)

    def columns(rows, i):
        return pl.BlockSpec((rows, DH), lambda h: (0, i * nh + h))

    return pl.pallas_call(
        body,
        grid=(nh,),
        in_specs=[columns(SEG, 0)] * SLOTS
        + [columns(SEG, 1)] * SLOTS
        + [columns(keyset.shape[0], i) for keyset in keysets for i in range(4)]
        + [ANY] * len(after),
        out_specs=[columns(OUT_ROWS, 0)] * SLOTS,
        out_shape=[jax.ShapeDtypeStruct((OUT_ROWS, nh * DH), jnp.bfloat16)] * SLOTS,
        compiler_params=pltpu.CompilerParams(vmem_limit_bytes=20 * MIB),
        cost_estimate=pl.CostEstimate(
            flops=nh * 2 * 16 * BLK * 3 * BLK * DH // 2,
            bytes_accessed=nh * 2_500_000,
            transcendentals=nh * 3 * BLK * BLK,
        ),
        name="attention",
    )(*messages, *messages, *[keyset for keyset in keysets for _ in range(4)], *after)


def unpack(chunks, plan):
    def body(*refs):
        chips = [slot_chip(k) for k in range(SLOTS)]
        parts, (att, att_tan, log_total, log_total_tan) = refs[: SLOTS * len(plan)], refs[SLOTS * len(plan) : -1]
        lines = refs[-1]
        for c, (base, nh) in enumerate(plan):
            for k in range(SLOTS):
                ref = parts[c * SLOTS + k]
                head = base + chips[k] * nh
                cols = pl.ds(pl.multiple_of(head * DH, DH), nh * DH)
                att[:, cols] = ref[0:SEG, :]
                att_tan[:, cols] = ref[SEG : 2 * SEG, :]
                stat = ref[2 * SEG : OUT_ROWS, :].astype(jnp.float32)
                stat = stat[0:2] + (stat[2:4] + stat[4:6])
                for j in range(nh):
                    lines[0, pl.ds(head + j, 1), :] = stat[0:1, j * DH : (j + 1) * DH]
                    lines[1, pl.ds(head + j, 1), :] = stat[1:2, j * DH : (j + 1) * DH]
        log_total[...] = lines[0]
        log_total_tan[...] = lines[1]

    heads = SLOTS * sum(nh for _, nh in plan)
    whole = pl.BlockSpec(memory_space=pltpu.VMEM)
    return pl.pallas_call(
        body,
        in_specs=[whole] * (SLOTS * len(plan)),
        out_specs=[whole] * 4,
        out_shape=[
            jax.ShapeDtypeStruct((SEG, heads * DH), jnp.bfloat16),
            jax.ShapeDtypeStruct((SEG, heads * DH), jnp.bfloat16),
            jax.ShapeDtypeStruct((heads, SEG), jnp.float32),
            jax.ShapeDtypeStruct((heads, SEG), jnp.float32),
        ],
        scratch_shapes=[pltpu.VMEM((2, heads, SEG), jnp.float32)],
        compiler_params=pltpu.CompilerParams(vmem_limit_bytes=16 * MIB),
        cost_estimate=pl.CostEstimate(flops=0, bytes_accessed=4 * SEG * heads * DH * 2, transcendentals=0),
        name="unpack",
    )(*chunks)


def per_device(queries, keys, values, queries_tan, keys_tan, values_tan):
    arrays = (queries_tan, queries, keys, keys_tan, values, values_tan)
    length = lax.axis_size("z") * lax.axis_size("x")
    there = [slot_pairs(k) for k in range(SLOTS)]
    back = [[(b, a) for a, b in pairs] for pairs in there]
    plan, base = [], 0
    for nh in CHUNKS:
        plan.append((base, nh))
        base += SLOTS * nh
    n = len(plan)
    arrived, joined, others, returned = [], [None] * n, [None] * n, [None] * n
    last = []
    for kind, c in ORDER:
        if kind == "pack":
            m, k = len(arrived), len(arrived) % SLOTS
            base, nh = plan[m // SLOTS]
            after = last + ([arrived[m - WINDOW]] if m >= WINDOW else [])
            sent = pack(arrays, base, nh, k, after)
            arrived.append(lax.ppermute(sent, RING, there[k]))
            last = [sent]
            continue
        base, nh = plan[c]
        messages = arrived[SLOTS * c : SLOTS * c + SLOTS]
        if kind == "join":
            joined[c] = join(messages, nh, last)
            outer = lax.ppermute(joined[c], LINE, outer_pairs(length))
            if GATHER:
                others[c] = (lax.all_gather(joined[c], "core", axis=0, tiled=True), outer)
            else:
                others[c] = (joined[c], lax.ppermute(joined[c], "core", [(0, 1), (1, 0)]), outer)
            last = [joined[c]]
        else:
            outs = attention(messages, others[c], nh, last)
            returned[c] = [lax.ppermute(outs[k], RING, back[k]) for k in range(SLOTS)]
            last = [outs[0]]
    att, att_tan, log_total, log_total_tan = unpack([part for parts in returned for part in parts], plan)
    return att, att_tan, log_total.T, log_total_tan.T


def solution(mesh):
    inner = Mesh(mesh.devices.reshape(2, 2, 8, 4, 2), AXES)
    placed = P(AXES, None)
    return jax.shard_map(
        per_device,
        mesh=inner,
        in_specs=(placed,) * 6,
        out_specs=(placed,) * 4,
        check_vma=False,
    )
```

```python
import functools

import jax
import jax.numpy as jnp
from jax import lax
from jax.experimental import pallas as pl
from jax.experimental.pallas import tpu as pltpu
from jax.sharding import Mesh, PartitionSpec as P

DH = 128
SEG = 128
BLK = 512
ROWS = 256
PAIR = 2
SLOTS = 4
OUT_ROWS = 2 * SEG + 16
SCALE = 1.0 / DH**0.5
LOG2E = 1.4426950408889634
AXES = ("y_hi", "core", "z", "x", "y_lo")
RING = ("y_hi", "core", "y_lo")
LINE = ("core", "z", "x")
STEPS = ((1, 2, 3, 0), (2, 3, 0, 1))
CHUNKS = (4, 4, 2)
WINDOW = 4
ORDER = (
    ("pack", 0, ()),
    ("pack", 0, ()),
    ("pack", 0, ()),
    ("pack", 0, ()),
    ("pack", 1, ()),
    ("pack", 1, ()),
    ("pack", 1, ()),
    ("pack", 1, ()),
    ("join", 0, ()),
    ("pack", 2, ()),
    ("pack", 2, ()),
    ("pack", 2, ()),
    ("pack", 2, ()),
    ("join", 1, ()),
    ("attend", 0, ()),
    ("join", 2, (1,)),
    ("attend", 1, ()),
    ("attend", 2, ()),
)
ANY = pl.BlockSpec(memory_space=pl.ANY)
HBM = pl.BlockSpec(memory_space=pltpu.HBM)
VMEM = pl.BlockSpec(memory_space=pltpu.VMEM)
MIB = 1024 * 1024


def slot_chip(k):
    y = 2 * lax.axis_index("y_hi") + lax.axis_index("y_lo")
    return (y + jnp.where(lax.axis_index("core") == 0, STEPS[0][k], STEPS[1][k])) % 4


def slot_pairs(k):
    pairs = []
    for y_hi in range(2):
        for core in range(2):
            for y_lo in range(2):
                y = (2 * y_hi + y_lo + STEPS[core][k]) % 4
                pairs.append((4 * y_hi + 2 * core + y_lo, 4 * (y // 2) + 2 * y_lo + y % 2))
    return pairs


def outer_pairs(length):
    return [(length + s, (s + 1) % length) for s in range(length)] + [
        (s, length + (s - 1) % length) for s in range(length)
    ]


def pack(arrays, base, nh, k, after):
    width = nh * DH

    def body(*refs):
        ins, (out, held, into, out_of) = refs[:6], refs[6 + len(after) :]
        first = pl.multiple_of((base + slot_chip(k) * nh) * DH, DH)
        loads = []
        for i, ref in enumerate(ins):
            load = pltpu.make_async_copy(
                ref.at[:, pl.ds(first, width)], held.at[:, pl.ds(i * width, width)], into.at[i]
            )
            load.start()
            loads.append(load)
        for load in loads:
            load.wait()
        store = pltpu.make_async_copy(held, out, out_of)
        store.start()
        store.wait()

    return pl.pallas_call(
        body,
        in_specs=[HBM] * 6 + [ANY] * len(after),
        out_specs=ANY,
        out_shape=jax.ShapeDtypeStruct((SEG, 6 * width), jnp.bfloat16),
        scratch_shapes=[
            pltpu.VMEM((SEG, 6 * width), jnp.bfloat16),
            pltpu.SemaphoreType.DMA((6,)),
            pltpu.SemaphoreType.DMA,
        ],
        compiler_params=pltpu.CompilerParams(vmem_limit_bytes=(16 if base else 60) * MIB),
        cost_estimate=pl.CostEstimate(flops=0, bytes_accessed=24 * SEG * width, transcendentals=0),
        name="pack",
    )(*arrays, *after)


def join(messages, nh, after):
    width = 4 * nh * DH

    def body(*refs):
        out = refs[-1]
        for k in range(SLOTS):
            out[k * SEG : (k + 1) * SEG, :] = refs[k][:, 2 * nh * DH :]

    return pl.pallas_call(
        body,
        in_specs=[VMEM] * SLOTS + [ANY] * len(after),
        out_specs=VMEM,
        out_shape=jax.ShapeDtypeStruct((BLK, width), jnp.bfloat16),
        compiler_params=pltpu.CompilerParams(vmem_limit_bytes=16 * MIB),
        cost_estimate=pl.CostEstimate(flops=0, bytes_accessed=4 * BLK * width, transcendentals=0),
        name="join",
    )(*messages, *after)


def score_rows(plain_q, joined_q, key_refs, cols):
    nt = (((1,), (1,)), ((), ()))
    scores, tangents = [], []
    for k, dk, v, dv in key_refs:
        plain_k = k[:, cols]
        joined_k = jnp.concatenate([plain_k, dk[:, cols]], axis=1)
        scores.append(lax.dot_general(plain_q, plain_k, nt, preferred_element_type=jnp.float32))
        tangents.append(lax.dot_general(joined_q, joined_k, nt, preferred_element_type=jnp.float32))
    return scores, tangents


def weigh_rows(scores, tangents, key_refs, cols):
    top = functools.reduce(jnp.maximum, [jnp.max(s, axis=-1, keepdims=True) for s in scores])
    expo = [jnp.exp2((s - top) * (SCALE * LOG2E)) for s in scores]
    total = sum(jnp.sum(e, axis=-1, keepdims=True) for e in expo)
    inverse = 1.0 / total
    mean = sum(jnp.sum(e * t, axis=-1, keepdims=True) for e, t in zip(expo, tangents)) * inverse
    both = jnp.zeros((ROWS, 2 * DH), jnp.float32)
    slope = jnp.zeros((ROWS, DH), jnp.float32)
    for (k, dk, v, dv), e, t in zip(key_refs, expo, tangents):
        probs = e * inverse
        low = probs.astype(jnp.bfloat16)
        tan_low = (probs * (t - mean)).astype(jnp.bfloat16)
        joined_v = jnp.concatenate([v[:, cols], dv[:, cols]], axis=1)
        both = both + jnp.dot(low, joined_v, preferred_element_type=jnp.float32)
        slope = slope + jnp.dot(tan_low, v[:, cols], preferred_element_type=jnp.float32)
    attended = both[:, :DH]
    attended_tan = both[:, DH:] + slope * SCALE
    log_total = top * SCALE + jnp.log(total)
    log_total_tan = mean * SCALE
    return attended, attended_tan, log_total, log_total_tan


def split3(x):
    high = x.astype(jnp.bfloat16)
    rest = x - high.astype(jnp.float32)
    middle = rest.astype(jnp.bfloat16)
    low = (rest - middle.astype(jnp.float32)).astype(jnp.bfloat16)
    return high, middle, low


def attention(messages, keysets, nh, after):
    def body(*refs):
        tan_refs, q_refs, refs = refs[:SLOTS], refs[SLOTS : 2 * SLOTS], refs[2 * SLOTS :]
        key_refs = [refs[4 * i : 4 * i + 4] for i in range(len(keysets))]
        outs = refs[4 * len(keysets) + len(after) :]
        per = ROWS // SEG
        units = [(j, part) for j in range(PAIR) for part in range(BLK // ROWS)]

        def products(j, part):
            cols = slice(j * DH, (j + 1) * DH)
            here = range(part * per, part * per + per)
            plain_q = jnp.concatenate([q_refs[k][:, cols] for k in here], axis=0)
            tan_q = jnp.concatenate([tan_refs[k][:, cols] for k in here], axis=0)
            return score_rows(plain_q, jnp.concatenate([tan_q, plain_q], axis=1), key_refs, cols)

        ready = products(*units[0])
        for u, (j, part) in enumerate(units):
            cols = slice(j * DH, (j + 1) * DH)
            held = ready
            if u + 1 < len(units):
                ready = products(*units[u + 1])
            attended, attended_tan, log_total, log_total_tan = weigh_rows(*held, key_refs, cols)
            lane = lax.broadcasted_iota(jnp.int32, (ROWS, DH), 1)
            stats = jnp.where(lane == 0, log_total, jnp.where(lane == 1, log_total_tan, 0.0))
            pieces = [piece.astype(jnp.float32) for piece in split3(stats)]
            for s in range(per):
                k = part * per + s
                rows = slice(s * SEG, (s + 1) * SEG)
                outs[k][0:SEG, cols] = attended[rows].astype(jnp.bfloat16)
                outs[k][SEG : 2 * SEG, cols] = attended_tan[rows].astype(jnp.bfloat16)
                lines = [piece[rows].T[0:2] for piece in pieces]
                lines.append(jnp.zeros((10, SEG), jnp.float32))
                outs[k][2 * SEG : OUT_ROWS, cols] = jnp.concatenate(lines, axis=0).astype(jnp.bfloat16)

    def columns(rows, i):
        return pl.BlockSpec((rows, PAIR * DH), lambda h: (0, i * (nh // PAIR) + h))

    return pl.pallas_call(
        body,
        grid=(nh // PAIR,),
        in_specs=[columns(SEG, 0)] * SLOTS
        + [columns(SEG, 1)] * SLOTS
        + [columns(keyset.shape[0], i) for keyset in keysets for i in range(4)]
        + [ANY] * len(after),
        out_specs=[columns(OUT_ROWS, 0)] * SLOTS,
        out_shape=[jax.ShapeDtypeStruct((OUT_ROWS, nh * DH), jnp.bfloat16)] * SLOTS,
        compiler_params=pltpu.CompilerParams(vmem_limit_bytes=28 * MIB),
        cost_estimate=pl.CostEstimate(
            flops=nh * 2 * 16 * BLK * 3 * BLK * DH // 2,
            bytes_accessed=nh * 2_500_000,
            transcendentals=nh * 3 * BLK * BLK,
        ),
        name="attention",
    )(*messages, *messages, *[keyset for keyset in keysets for _ in range(4)], *after)


def unpack(chunks, plan):
    def body(*refs):
        chips = [slot_chip(k) for k in range(SLOTS)]
        parts, (att, att_tan, log_total, log_total_tan) = refs[: SLOTS * len(plan)], refs[SLOTS * len(plan) : -1]
        lines = refs[-1]
        for c, (base, nh) in enumerate(plan):
            for k in range(SLOTS):
                ref = parts[c * SLOTS + k]
                head = base + chips[k] * nh
                cols = pl.ds(pl.multiple_of(head * DH, DH), nh * DH)
                att[:, cols] = ref[0:SEG, :]
                att_tan[:, cols] = ref[SEG : 2 * SEG, :]
                stat = ref[2 * SEG : OUT_ROWS, :].astype(jnp.float32)
                stat = stat[0:2] + (stat[2:4] + stat[4:6])
                for j in range(nh):
                    lines[0, pl.ds(head + j, 1), :] = stat[0:1, j * DH : (j + 1) * DH]
                    lines[1, pl.ds(head + j, 1), :] = stat[1:2, j * DH : (j + 1) * DH]
        log_total[...] = lines[0]
        log_total_tan[...] = lines[1]

    heads = SLOTS * sum(nh for _, nh in plan)
    whole = pl.BlockSpec(memory_space=pltpu.VMEM)
    return pl.pallas_call(
        body,
        in_specs=[whole] * (SLOTS * len(plan)),
        out_specs=[whole] * 4,
        out_shape=[
            jax.ShapeDtypeStruct((SEG, heads * DH), jnp.bfloat16),
            jax.ShapeDtypeStruct((SEG, heads * DH), jnp.bfloat16),
            jax.ShapeDtypeStruct((heads, SEG), jnp.float32),
            jax.ShapeDtypeStruct((heads, SEG), jnp.float32),
        ],
        scratch_shapes=[pltpu.VMEM((2, heads, SEG), jnp.float32)],
        compiler_params=pltpu.CompilerParams(vmem_limit_bytes=16 * MIB),
        cost_estimate=pl.CostEstimate(flops=0, bytes_accessed=4 * SEG * heads * DH * 2, transcendentals=0),
        name="unpack",
    )(*chunks)


def per_device(queries, keys, values, queries_tan, keys_tan, values_tan):
    arrays = (queries_tan, queries, keys, keys_tan, values, values_tan)
    length = lax.axis_size("z") * lax.axis_size("x")
    there = [slot_pairs(k) for k in range(SLOTS)]
    back = [[(b, a) for a, b in pairs] for pairs in there]
    plan, base = [], 0
    for nh in CHUNKS:
        plan.append((base, nh))
        base += SLOTS * nh
    n = len(plan)
    arrived, joined, others, returned = [], [None] * n, [None] * n, [None] * n
    last = []
    for kind, c, seen in ORDER:
        last = last + [array for i in seen for array in others[i][1:]]
        if kind == "pack":
            m, k = len(arrived), len(arrived) % SLOTS
            base, nh = plan[m // SLOTS]
            after = last + ([arrived[m - WINDOW]] if m >= WINDOW else [])
            sent = pack(arrays, base, nh, k, after)
            arrived.append(lax.ppermute(sent, RING, there[k]))
            last = [sent]
            continue
        base, nh = plan[c]
        messages = arrived[SLOTS * c : SLOTS * c + SLOTS]
        if kind == "join":
            joined[c] = join(messages, nh, last)
            outer = lax.ppermute(joined[c], LINE, outer_pairs(length))
            others[c] = (joined[c], lax.ppermute(joined[c], "core", [(0, 1), (1, 0)]), outer)
            last = [joined[c]]
        else:
            outs = attention(messages, others[c], nh, last)
            returned[c] = [lax.ppermute(outs[k], RING, back[k]) for k in range(SLOTS)]
            last = [outs[0]]
    att, att_tan, log_total, log_total_tan = unpack([part for parts in returned for part in parts], plan)
    return att, att_tan, log_total.T, log_total_tan.T


def solution(mesh):
    inner = Mesh(mesh.devices.reshape(2, 2, 8, 4, 2), AXES)
    placed = P(AXES, None)
    return jax.shard_map(
        per_device,
        mesh=inner,
        in_specs=(placed,) * 6,
        out_specs=(placed,) * 4,
        check_vma=False,
    )
```
